512 devices in a mesh: fsdp: 128 (over x, z_hi, y, core), seq: 4 (over z_lo).
Axes of the slice: x: 4, y: 4, z: 16 (z_hi: 4, z_lo: 4; z = z_hi * 4 + z_lo), core: 2. Of those that a mesh axis runs over, the one named last changes fastest.
Arguments:
- query_frames: bfloat16 [16, 4096, 2048], P('seq', 'fsdp'), may hold values from -6 to 6
- key_frames: bfloat16 [16, 4096, 2048], P('seq', 'fsdp'), may hold values from -6 to 6
- value_frames: bfloat16 [16, 4096, 2048], P('seq', 'fsdp'), may hold values from -24 to 24
- out_weight: bfloat16 [2048, 2048], P('fsdp', 'seq'), may hold values from -0.125 to 0.125
- out_grad: bfloat16 [16, 4096, 2048], P(None, 'fsdp', 'seq'), may hold values from -1.5 to 1.5
Outputs:
- block_out: bfloat16 [16, 4096, 2048], P(None, 'fsdp', 'seq')
- query_grad: bfloat16 [16, 4096, 2048], P('seq', 'fsdp')
- key_grad: bfloat16 [16, 4096, 2048], P('seq', 'fsdp')
- value_grad: bfloat16 [16, 4096, 2048], P('seq', 'fsdp')
- weight_grad: float32 [2048, 2048], P('fsdp', 'seq')
The draws below stay inside these ranges and needn't reach their ends.
All inputs are finite; a program needn't handle non-finite values.
Results may differ from the reference program's by a relative error of at most 0.0058.
Values may be sent and summed in bfloat16 or wider, within the bound.
No kernel may reach another device: no remote copies, remote signals or barrier semaphores. Data moves between devices by JAX's collectives and lax.ppermute only.
A program may use at most 64 MiB of HBM per device.

```python
import math
import jax
import jax.numpy as jnp
from jax import lax

D = 2048
HEADS = 16
HD = 128
FRAMES = 16
HW = 2048
PIXELS = 4096


def draw_query_frames(key, part):
    key = jax.random.fold_in(key, 1)
    shape = (FRAMES, PIXELS, HEADS * HD)
    return jnp.clip(jax.random.normal(key, shape, jnp.float32), -6.0, 6.0).astype(jnp.bfloat16)


def draw_key_frames(key, part):
    key = jax.random.fold_in(key, 2)
    shape = (FRAMES, PIXELS, HEADS * HD)
    return jnp.clip(jax.random.normal(key, shape, jnp.float32), -6.0, 6.0).astype(jnp.bfloat16)


def with_spikes(values, own_key, source, target, blocks, factor):
    owner, partner = [(jnp.arange(values.shape[position]) // (values.shape[position] // blocks)).reshape([-1 if axis == position else 1 for axis in range(values.ndim)]) for position in (source, target)]
    chosen = jax.random.permutation(own_key, blocks)[partner]
    strong = (owner == chosen) | (owner == (partner + blocks // 2) % blocks)
    return jnp.where(strong, factor * values, values)


def block_scale(stream_key, shape, split, smallest, top_value):
    level, own = 1.0, jax.random.fold_in(stream_key, 6)
    for position, blocks in split:
        draws = jnp.exp(jax.random.uniform(jax.random.fold_in(own, position), (blocks,), jnp.float32, smallest / len(split), top_value / len(split)))
        level = level * jnp.repeat(draws, shape[position] // blocks).reshape([-1 if axis == position else 1 for axis in range(len(shape))])
    return level


def centred(rng, dims, deviation, limit, pieces=(), kind=jnp.bfloat16):
    drawn = deviation * jax.random.normal(rng, dims, jnp.float32)
    if pieces:
        drawn = drawn * block_scale(rng, dims, pieces, -0.22, 0.18)
    return jnp.clip(drawn, -limit, limit).astype(kind)


def bell_draw_with(own_key, extent, spread, limit, shards, heavy, kind=jnp.bfloat16):
    drawn = spread * jax.random.normal(own_key, extent, jnp.float32)
    if shards:
        drawn = drawn * block_scale(own_key, extent, shards, -0.22, 0.18)
    return jnp.clip(with_spikes(drawn, jax.random.fold_in(own_key, 3), *heavy), -limit, limit).astype(kind)


def setup_inputs(seed: int = 0) -> dict:
    arg_keys = jax.random.split(jax.random.key(seed), 6)
    query_frames = draw_query_frames(jax.random.fold_in(arg_keys[5], 71), 0)
    key_frames = draw_key_frames(jax.random.fold_in(arg_keys[5], 71), 0)
    value_frames = bell_draw_with(arg_keys[2], (FRAMES, PIXELS, HW), 1.0, 24.0, ((0, 4), (1, 128)), (1, 2, 128, 5.5))
    out_weight = centred(arg_keys[3], (HW, D), HW ** -0.5, 0.125, ((0, 128), (1, 4)))
    out_grad = centred(arg_keys[4], (FRAMES, PIXELS, D), 0.25, 1.5, ((1, 128), (2, 4)))
    return dict(query_frames=query_frames, key_frames=key_frames, value_frames=value_frames, out_weight=out_weight, out_grad=out_grad)


def causal_weights(query_heads, key_heads):
    frames = query_heads.shape[0]
    scores = jnp.einsum('tphd,sphd->phts', query_heads, key_heads) * (1.0 / math.sqrt(HD))
    allowed = lax.broadcasted_iota(jnp.int32, (frames, frames), 0) >= lax.broadcasted_iota(jnp.int32, (frames, frames), 1)
    scores = jnp.where(allowed, scores, -1e+30)
    peak_score = lax.optimization_barrier(jnp.max(scores, axis=-1, keepdims=True))
    expo_terms = jnp.exp(scores - peak_score)
    return expo_terms / lax.optimization_barrier(jnp.sum(expo_terms, axis=-1, keepdims=True))

def split_heads(array):
    return array.reshape(array.shape[0], array.shape[1], -1, HD).astype(jnp.float32)

def forward_block(triple):
    query_part, key_part, value_part = triple
    query_heads = split_heads(query_part)
    key_heads = split_heads(key_part)
    value_heads = split_heads(value_part)
    weights = causal_weights(query_heads, key_heads)
    rounded = lax.optimization_barrier(weights.astype(jnp.bfloat16)).astype(jnp.float32)
    attended = jnp.einsum('phts,sphd->tphd', rounded, value_heads)
    return attended.reshape(query_part.shape).astype(jnp.bfloat16)

def backward_block(quad):
    query_part, key_part, value_part, grad_part = quad
    query_heads = split_heads(query_part)
    key_heads = split_heads(key_part)
    value_heads = split_heads(value_part)
    grad_heads = split_heads(grad_part)
    weights = causal_weights(query_heads, key_heads)
    rounded = lax.optimization_barrier(weights.astype(jnp.bfloat16)).astype(jnp.float32)
    value_grad = jnp.einsum('phts,tphd->sphd', rounded, grad_heads)
    weights_grad = jnp.einsum('tphd,sphd->phts', grad_heads, value_heads)
    scores_grad = weights * (weights_grad - lax.optimization_barrier(jnp.sum(weights * weights_grad, axis=-1, keepdims=True)))
    scaled = lax.optimization_barrier((scores_grad * (1.0 / math.sqrt(HD))).astype(jnp.bfloat16)).astype(jnp.float32)
    query_grad = jnp.einsum('phts,sphd->tphd', scaled, key_heads)
    key_grad = jnp.einsum('phts,tphd->sphd', scaled, query_heads)
    shape = query_part.shape
    return (query_grad.reshape(shape).astype(jnp.bfloat16), key_grad.reshape(shape).astype(jnp.bfloat16), value_grad.reshape(shape).astype(jnp.bfloat16))

def reference(query_frames, key_frames, value_frames, out_weight, out_grad):
    width = HEADS * HD
    block = math.gcd(PIXELS, 256)
    blocks = PIXELS // block

    def to_blocks(array):
        return array.reshape(FRAMES, blocks, block, array.shape[-1]).transpose(1, 0, 2, 3)

    def from_blocks(array):
        return array.transpose(1, 0, 2, 3).reshape(FRAMES, PIXELS, array.shape[-1])
    attended = from_blocks(lax.map(forward_block, (to_blocks(query_frames), to_blocks(key_frames), to_blocks(value_frames))))
    flat_attended = attended.reshape(FRAMES * PIXELS, width)
    flat_grad = out_grad.reshape(FRAMES * PIXELS, D)
    block_out = jnp.dot(flat_attended, out_weight, preferred_element_type=jnp.float32).astype(jnp.bfloat16).reshape(FRAMES, PIXELS, D)
    attended_grad = jnp.dot(flat_grad, out_weight.T, preferred_element_type=jnp.float32).astype(jnp.bfloat16).reshape(FRAMES, PIXELS, width)
    weight_grad = jnp.dot(flat_attended.T, flat_grad, preferred_element_type=jnp.float32)
    grads = lax.map(backward_block, (to_blocks(query_frames), to_blocks(key_frames), to_blocks(value_frames), to_blocks(attended_grad)))
    query_grad = from_blocks(grads[0])
    key_grad = from_blocks(grads[1])
    value_grad = from_blocks(grads[2])
    return (block_out, query_grad, key_grad, value_grad, weight_grad)
```

```python
import functools
import math

import jax
import jax.numpy as jnp
from jax import lax
from jax.experimental import pallas as pl
from jax.experimental.pallas import tpu as pltpu
from jax.sharding import Mesh
from jax.sharding import PartitionSpec as P

HD = 128
SCALE = 1.0 / math.sqrt(HD)
BF = jnp.bfloat16
F32 = jnp.float32
VMEM = pl.BlockSpec(memory_space=pltpu.VMEM)
SMEM = pl.BlockSpec(memory_space=pltpu.SMEM)
ANY = pl.BlockSpec(memory_space=pl.ANY)
NT = (((1,), (1,)), ((), ()))
TN = (((0,), (0,)), ((), ()))
NN = (((1,), (0,)), ((), ()))
X, ZH, Y, C, S = range(5)
DEVICES = ("x", "zh", "y", "c", "s")


def dot(a, b, dims):
    return lax.dot_general(a, b, dims, preferred_element_type=F32)


def shift(array, axis, step):
    return lax.ppermute(array, axis, [(i, (i + step) % 4) for i in range(4)])


def params(mib):
    return pltpu.CompilerParams(vmem_limit_bytes=mib * 2**20)


def wrap(index, step):
    return lax.rem(index + step, 4)


def run_copies(pairs, sems):
    copies = [pltpu.make_async_copy(src, dst, sems.at[n]) for n, (src, dst) in enumerate(pairs)]
    for copy in copies:
        copy.start()
    return copies


def wait_all(copies):
    for copy in copies:
        copy.wait()


def pack_kernel(pos_ref, q_ref, k_ref, v_ref, g_ref, o0, o1, o2, o3, rows_ref, grad_ref, wide_ref, sems):
    pairs = [(ref, rows_ref.at[which]) for which, ref in enumerate((q_ref, k_ref, v_ref))]
    copies = run_copies(pairs + [(g_ref, grad_ref)], sems)
    for which in range(4):
        copies[which].wait()
        for part in range(4):
            lanes = slice(512 * part, 512 * part + 512)
            block = rows_ref[which, :, :, lanes] if which < 3 else grad_ref[4 * part : 4 * part + 4]
            wide_ref[part] = block.astype(F32)
            for step, out in enumerate((o0, o1, o2, o3)):
                pixels = pl.ds(pl.multiple_of(wrap(pos_ref[S], step) * 8, 8), 8)
                out[which, :, lanes] = wide_ref[part, :, pixels, :].reshape(32, 512).astype(BF)


def unpack_kernel(pos_ref, h0, h1, h2, h3, q_ref, k_ref, v_ref, rows_ref, wide_ref, sems):
    copies = run_copies([(ref, rows_ref.at[step]) for step, ref in enumerate((h0, h1, h2, h3))], sems)
    wait_all(copies)
    for which, out in enumerate((q_ref, k_ref, v_ref)):
        for part in range(4):
            lanes = slice(512 * part, 512 * part + 512)
            for step in range(4):
                pixels = pl.ds(pl.multiple_of(wrap(pos_ref[S], 4 - step) * 8, 8), 8)
                wide_ref[part, :, pixels, :] = rows_ref[step, which, :, lanes].astype(F32).reshape(4, 8, 512)
            out[:, :, lanes] = wide_ref[part].astype(BF)


def allowed_pairs():
    row = lax.broadcasted_iota(jnp.int32, (128, 128), 0)
    col = lax.broadcasted_iota(jnp.int32, (128, 128), 1)
    return ((row & 7) == (col & 7)) & (col <= row)


def softmax_heads(qs, ks, allowed):
    scores = [jnp.where(allowed, dot(q, k, NT) * SCALE, -1e30) for q, k in zip(qs, ks)]
    peaks = [jnp.max(s, axis=-1, keepdims=True) for s in scores]
    terms = [jnp.exp(s - p) for s, p in zip(scores, peaks)]
    sums = [jnp.sum(t, axis=-1, keepdims=True) for t in terms]
    return [t / s for t, s in zip(terms, sums)]


def heads_of(all_ref, which, heads):
    return [all_ref[which, :, :, 128 * h : 128 * h + 128].reshape(128, 128) for h in heads]


def inputs_of(pos_ref, pieces, all_ref):
    return [(ref.at[0:3], all_ref.at[:, wrap(pos_ref[S], 4 - step)]) for step, ref in enumerate(pieces)]


def forward_kernel(pos_ref, e0, e1, e2, e3, att_ref, all_ref, sems):
    wait_all(run_copies(inputs_of(pos_ref, (e0, e1, e2, e3), all_ref), sems))
    allowed = allowed_pairs()
    for block in range(4):
        heads = [4 * block + i for i in range(4)]
        qs, ks, vs = (heads_of(all_ref, which, heads) for which in range(3))
        weights = softmax_heads(qs, ks, allowed)
        for h, w, v in zip(heads, weights, vs):
            att_ref[:, 128 * h : 128 * h + 128] = dot(w.astype(BF), v, NN).astype(BF)


def backward_kernel(
    pos_ref, e0, e1, e2, e3, mine_ref, other_ref, f0, f1, f2, f3, w_ref, all_ref, grad_ref, ag_ref, sems, out_sems
):
    pieces = (e0, e1, e2, e3)
    pairs = []
    for core, ref in enumerate((mine_ref, other_ref)):
        c = pos_ref[C] if core == 0 else 1 - pos_ref[C]
        pairs += [(ref.at[:, :, s, zh], w_ref.at[s, :, zh, :, c]) for s in range(4) for zh in range(4)]
    for step, ref in enumerate(pieces):
        lanes = pl.ds(pl.multiple_of(wrap(pos_ref[S], 4 - step) * 512, 512), 512)
        pairs += [(ref.at[3, :, 512 * g : 512 * g + 512], grad_ref.at[g, :, lanes]) for g in range(4)]
    pairs += inputs_of(pos_ref, pieces, all_ref)
    wait_all(run_copies(pairs, sems))
    total = None
    for s in range(4):
        rows = grad_ref[:, :, 512 * s : 512 * s + 512].reshape(128, 512)
        part = dot(rows, w_ref[s].reshape(2048, 512), NT)
        total = part if total is None else total + part
    ag_ref[...] = total.astype(BF)
    allowed = allowed_pairs()
    for block in range(4):
        heads = [4 * block + i for i in range(4)]
        qs, ks, vs = (heads_of(all_ref, which, heads) for which in range(3))
        gs = [ag_ref[:, 128 * h : 128 * h + 128] for h in heads]
        weights = softmax_heads(qs, ks, allowed)
        wgrads = [dot(g, v, NT) for g, v in zip(gs, vs)]
        dvs = [dot(w.astype(BF), g, TN) for w, g in zip(weights, gs)]
        means = [jnp.sum(w * d, axis=-1, keepdims=True) for w, d in zip(weights, wgrads)]
        sgrads = [(w * (d - m) * SCALE).astype(BF) for w, d, m in zip(weights, wgrads, means)]
        dqs = [dot(d, k, NN) for d, k in zip(sgrads, ks)]
        dks = [dot(d, q, TN) for d, q in zip(sgrads, qs)]
        for which, grads in enumerate((dqs, dks, dvs)):
            for h, grad in zip(heads, grads):
                all_ref[which, :, :, 128 * h : 128 * h + 128] = grad.astype(BF).reshape(4, 32, 128)
    pairs = [(all_ref.at[:, wrap(pos_ref[S], step)], out) for step, out in enumerate((f0, f1, f2, f3))]
    wait_all(run_copies(pairs, out_sems))


def weight_kernel(pos_ref, a0, a1, a2, a3, p0, p1, p2, p3, keep_ref, send_ref, att_ref, grad_ref, sum_ref, sems):
    pairs = [(ref, att_ref.at[step]) for step, ref in enumerate((a0, a1, a2, a3))]
    for step, ref in enumerate((p0, p3, p2, p1)):
        pairs += [(ref.at[3, :, 512 * g : 512 * g + 512], grad_ref.at[step, g]) for g in range(4)]
    wait_all(run_copies(pairs, sems))
    grads = grad_ref[...].reshape(512, 512)
    c = pos_ref[C]
    for block in range(4):
        att = att_ref[:, :, 512 * block : 512 * block + 512].reshape(512, 512)
        sum_ref[...] = dot(att, grads, TN).reshape(4, 4, 2, 16, 512)
        for zh in range(4):
            keep_ref[block, :, zh] = sum_ref[zh, :, c]
            send_ref[block, :, zh] = sum_ref[zh, :, 1 - c]


def output_kernel(pos_ref, a0, a1, a2, a3, mine_ref, other_ref, out_ref, w_ref, att_ref, wide_ref, sems):
    pairs = [(ref, att_ref.at[step]) for step, ref in enumerate((a0, a1, a2, a3))]
    for core, ref in enumerate((mine_ref, other_ref)):
        c = pos_ref[C] if core == 0 else 1 - pos_ref[C]
        pairs += [(ref.at[:, :, pos_ref[S], zh], w_ref.at[:, zh, :, c]) for zh in range(4)]
    wait_all(run_copies(pairs, sems))
    rows = dot(att_ref[...].reshape(512, 2048), w_ref[...].reshape(2048, 512), NN).reshape(4, 16, 8, 512)
    for step in range(4):
        pixels = pl.ds(pl.multiple_of(wrap(pos_ref[S], 4 - step) * 8, 8), 8)
        wide_ref[:, pixels, :] = rows[step]
    out_ref[...] = wide_ref[...].astype(BF)


def call(kernel, name, out_shape, inputs, out_spec, scratch, mib):
    return pl.pallas_call(
        kernel,
        out_shape=out_shape,
        in_specs=[SMEM] + [ANY] * (len(inputs) - 1),
        out_specs=jax.tree.map(lambda _: out_spec, out_shape),
        scratch_shapes=scratch,
        compiler_params=params(mib),
        name=name,
    )(*inputs)


def per_device(query_frames, key_frames, value_frames, out_weight, out_grad):
    pos = jnp.stack([lax.axis_index(a) for a in DEVICES]).astype(jnp.int32)
    swap = [(0, 1), (1, 0)]
    dma = pltpu.SemaphoreType.DMA

    spread = jnp.broadcast_to(out_weight[None], (16, 16, 512))
    column = lax.all_to_all(spread, ("s", "zh"), 0, 0)

    parcel = jax.ShapeDtypeStruct((4, 32, 2048), BF)
    sent = call(
        pack_kernel, "pack", [parcel] * 4, (pos, query_frames, key_frames, value_frames, out_grad), VMEM,
        [pltpu.VMEM((3, 4, 32, 2048), BF), pltpu.VMEM((16, 32, 512), BF), pltpu.VMEM((4, 4, 32, 512), F32), dma((4,))], 32,
    )
    column, sent = lax.optimization_barrier((column, sent))
    arrived = [sent[0]] + [shift(sent[n], "s", n) for n in (1, 2, 3)]
    mine = lax.all_gather(column.reshape(256, 512), ("x", "y"), axis=0, tiled=True).reshape(4, 4, 4, 4, 16, 512)

    attended = call(
        forward_kernel, "forward", jax.ShapeDtypeStruct((128, 2048), BF), (pos, *arrived), VMEM,
        [pltpu.VMEM((3, 4, 32, 2048), BF), dma((4,))], 24,
    )
    attended_all = [attended] + [shift(attended, "s", n) for n in (1, 2, 3)]
    mine, attended_all[1] = lax.optimization_barrier((mine, attended_all[1]))
    other = lax.ppermute(mine, "c", swap)

    back = call(
        backward_kernel, "backward", [jax.ShapeDtypeStruct((3, 32, 2048), BF)] * 4, (pos, *arrived, mine, other), ANY,
        [
            pltpu.VMEM((4, 4, 4, 4, 2, 16, 512), BF),
            pltpu.VMEM((3, 4, 32, 2048), BF),
            pltpu.VMEM((4, 32, 2048), BF),
            pltpu.VMEM((128, 2048), BF),
            dma((52,)),
            dma((4,)),
        ],
        40,
    )
    home = [back[0]] + [shift(back[n], "s", n) for n in (1, 2, 3)]

    home[1], *attended_all = lax.optimization_barrier((home[1], *attended_all))
    quarter = jax.ShapeDtypeStruct((4, 4, 4, 16, 512), F32)
    keep, send = call(
        weight_kernel, "weight", [quarter] * 2, (pos, *attended_all, *sent), VMEM,
        [
            pltpu.VMEM((4, 128, 2048), BF),
            pltpu.VMEM((4, 4, 32, 512), BF),
            pltpu.VMEM((4, 4, 2, 16, 512), F32),
            dma((20,)),
        ],
        32,
    )
    chip_sum = keep + lax.ppermute(send, "c", swap)
    parts = lax.all_to_all(chip_sum.reshape(16, 4, 16, 512), ("x", "y"), 0, 0)

    block_out = call(
        output_kernel, "project", jax.ShapeDtypeStruct((16, 32, 512), BF), (pos, *attended_all, mine, other), VMEM,
        [
            pltpu.VMEM((4, 4, 4, 2, 16, 512), BF),
            pltpu.VMEM((4, 128, 2048), BF),
            pltpu.VMEM((16, 32, 512), F32),
            dma((12,)),
        ],
        32,
    )
    query_grad, key_grad, value_grad = call(
        unpack_kernel, "unpack", [jax.ShapeDtypeStruct((4, 32, 2048), BF)] * 3, (pos, *home), VMEM,
        [pltpu.VMEM((4, 3, 32, 2048), BF), pltpu.VMEM((4, 4, 32, 512), F32), dma((4,))], 32,
    )
    parts, block_out, query_grad, key_grad, value_grad = lax.optimization_barrier(
        (parts, block_out, query_grad, key_grad, value_grad)
    )
    plane_sum = parts.sum(axis=0)
    weight_grad = None
    for step in range(4):
        part = lax.dynamic_index_in_dim(plane_sum, wrap(pos[ZH], step), 0, keepdims=False)
        got = part if step == 0 else shift(part, "zh", step)
        weight_grad = got if weight_grad is None else weight_grad + got
    return block_out, query_grad, key_grad, value_grad, weight_grad


def solution(mesh):
    fine = Mesh(mesh.devices.reshape(4, 4, 4, 2, 4), ("x", "zh", "y", "c", "s"))
    fsdp = ("x", "zh", "y", "c")
    return jax.shard_map(
        per_device,
        mesh=fine,
        in_specs=(
            P("s", fsdp, None),
            P("s", fsdp, None),
            P("s", fsdp, None),
            P(fsdp, "s"),
            P(None, fsdp, "s"),
        ),
        out_specs=(
            P(None, fsdp, "s"),
            P("s", fsdp, None),
            P("s", fsdp, None),
            P("s", fsdp, None),
            P(fsdp, "s"),
        ),
        check_vma=False,
    )
```

```python
import functools
import math

import jax
import jax.numpy as jnp
from jax import lax
from jax.experimental import pallas as pl
from jax.experimental.pallas import tpu as pltpu
from jax.sharding import Mesh
from jax.sharding import PartitionSpec as P

HD = 128
SCALE = 1.0 / math.sqrt(HD)
BF = jnp.bfloat16
F32 = jnp.float32
VMEM = pl.BlockSpec(memory_space=pltpu.VMEM)
SMEM = pl.BlockSpec(memory_space=pltpu.SMEM)
ANY = pl.BlockSpec(memory_space=pl.ANY)
NT = (((1,), (1,)), ((), ()))
TN = (((0,), (0,)), ((), ()))
NN = (((1,), (0,)), ((), ()))
X, ZH, Y, C, S = range(5)
DEVICES = ("x", "zh", "y", "c", "s")


def dot(a, b, dims):
    return lax.dot_general(a, b, dims, preferred_element_type=F32)


def shift(array, axis, step):
    return lax.ppermute(array, axis, [(i, (i + step) % 4) for i in range(4)])


def params(mib):
    return pltpu.CompilerParams(vmem_limit_bytes=mib * 2**20)


def wrap(index, step):
    return lax.rem(index + step, 4)


def run_copies(pairs, sems):
    copies = [pltpu.make_async_copy(src, dst, sems.at[n]) for n, (src, dst) in enumerate(pairs)]
    for copy in copies:
        copy.start()
    return copies


def wait_all(copies):
    for copy in copies:
        copy.wait()


def pack_kernel(pos_ref, q_ref, k_ref, v_ref, g_ref, o0, o1, o2, o3, rows_ref, grad_ref, wide_ref, sems):
    pairs = [(ref, rows_ref.at[which]) for which, ref in enumerate((q_ref, k_ref, v_ref))]
    copies = run_copies(pairs + [(g_ref, grad_ref)], sems)
    for which in range(4):
        copies[which].wait()
        for part in range(4):
            lanes = slice(512 * part, 512 * part + 512)
            block = rows_ref[which, :, :, lanes] if which < 3 else grad_ref[4 * part : 4 * part + 4]
            wide_ref[part] = block.astype(F32)
            for step, out in enumerate((o0, o1, o2, o3)):
                pixels = pl.ds(pl.multiple_of(wrap(pos_ref[S], step) * 8, 8), 8)
                out[which, :, lanes] = wide_ref[part, :, pixels, :].reshape(32, 512).astype(BF)


def unpack_kernel(pos_ref, h0, h1, h2, h3, q_ref, k_ref, v_ref, rows_ref, wide_ref, sems):
    copies = run_copies([(ref, rows_ref.at[step]) for step, ref in enumerate((h0, h1, h2, h3))], sems)
    wait_all(copies)
    for which, out in enumerate((q_ref, k_ref, v_ref)):
        for part in range(4):
            lanes = slice(512 * part, 512 * part + 512)
            for step in range(4):
                pixels = pl.ds(pl.multiple_of(wrap(pos_ref[S], 4 - step) * 8, 8), 8)
                wide_ref[part, :, pixels, :] = rows_ref[step, which, :, lanes].astype(F32).reshape(4, 8, 512)
            out[:, :, lanes] = wide_ref[part].astype(BF)


def allowed_pairs():
    row = lax.broadcasted_iota(jnp.int32, (128, 128), 0)
    col = lax.broadcasted_iota(jnp.int32, (128, 128), 1)
    return ((row & 7) == (col & 7)) & (col <= row)


def softmax_heads(qs, ks, allowed):
    scores = [jnp.where(allowed, dot(q, k, NT) * SCALE, -1e30) for q, k in zip(qs, ks)]
    peaks = [jnp.max(s, axis=-1, keepdims=True) for s in scores]
    terms = [jnp.exp(s - p) for s, p in zip(scores, peaks)]
    sums = [jnp.sum(t, axis=-1, keepdims=True) for t in terms]
    return [t / s for t, s in zip(terms, sums)]


def heads_of(all_ref, which, heads):
    return [all_ref[which, :, :, 128 * h : 128 * h + 128].reshape(128, 128) for h in heads]


def inputs_of(pos_ref, pieces, all_ref):
    return [(ref.at[0:3], all_ref.at[:, wrap(pos_ref[S], 4 - step)]) for step, ref in enumerate(pieces)]


def forward_kernel(pos_ref, e0, e1, e2, e3, att_ref, all_ref, sems):
    wait_all(run_copies(inputs_of(pos_ref, (e0, e1, e2, e3), all_ref), sems))
    allowed = allowed_pairs()
    for block in range(4):
        heads = [4 * block + i for i in range(4)]
        qs, ks, vs = (heads_of(all_ref, which, heads) for which in range(3))
        weights = softmax_heads(qs, ks, allowed)
        for h, w, v in zip(heads, weights, vs):
            att_ref[:, 128 * h : 128 * h + 128] = dot(w.astype(BF), v, NN).astype(BF)


def backward_kernel(
    pos_ref, e0, e1, e2, e3, mine_ref, other_ref, f0, f1, f2, f3, w_ref, all_ref, grad_ref, ag_ref, sems, out_sems
):
    pieces = (e0, e1, e2, e3)
    pairs = []
    for core, ref in enumerate((mine_ref, other_ref)):
        c = pos_ref[C] if core == 0 else 1 - pos_ref[C]
        pairs += [(ref.at[:, :, s, zh], w_ref.at[s, :, zh, :, c]) for s in range(4) for zh in range(4)]
    for step, ref in enumerate(pieces):
        lanes = pl.ds(pl.multiple_of(wrap(pos_ref[S], 4 - step) * 512, 512), 512)
        pairs += [(ref.at[3, :, 512 * g : 512 * g + 512], grad_ref.at[g, :, lanes]) for g in range(4)]
    pairs += inputs_of(pos_ref, pieces, all_ref)
    wait_all(run_copies(pairs, sems))
    total = None
    for s in range(4):
        rows = grad_ref[:, :, 512 * s : 512 * s + 512].reshape(128, 512)
        part = dot(rows, w_ref[s].reshape(2048, 512), NT)
        total = part if total is None else total + part
    ag_ref[...] = total.astype(BF)
    allowed = allowed_pairs()
    for block in range(4):
        heads = [4 * block + i for i in range(4)]
        qs, ks, vs = (heads_of(all_ref, which, heads) for which in range(3))
        gs = [ag_ref[:, 128 * h : 128 * h + 128] for h in heads]
        weights = softmax_heads(qs, ks, allowed)
        wgrads = [dot(g, v, NT) for g, v in zip(gs, vs)]
        dvs = [dot(w.astype(BF), g, TN) for w, g in zip(weights, gs)]
        means = [jnp.sum(w * d, axis=-1, keepdims=True) for w, d in zip(weights, wgrads)]
        sgrads = [(w * (d - m) * SCALE).astype(BF) for w, d, m in zip(weights, wgrads, means)]
        dqs = [dot(d, k, NN) for d, k in zip(sgrads, ks)]
        dks = [dot(d, q, TN) for d, q in zip(sgrads, qs)]
        for which, grads in enumerate((dqs, dks, dvs)):
            for h, grad in zip(heads, grads):
                all_ref[which, :, :, 128 * h : 128 * h + 128] = grad.astype(BF).reshape(4, 32, 128)
    pairs = [(all_ref.at[:, wrap(pos_ref[S], step)], out) for step, out in enumerate((f0, f1, f2, f3))]
    wait_all(run_copies(pairs, out_sems))


def weight_kernel(pos_ref, a0, a1, a2, a3, p0, p1, p2, p3, keep_ref, send_ref, att_ref, grad_ref, sum_ref, sems):
    pairs = [(ref, att_ref.at[step]) for step, ref in enumerate((a0, a1, a2, a3))]
    for step, ref in enumerate((p0, p3, p2, p1)):
        pairs += [(ref.at[3, :, 512 * g : 512 * g + 512], grad_ref.at[step, g]) for g in range(4)]
    wait_all(run_copies(pairs, sems))
    grads = grad_ref[...].reshape(512, 512)
    c = pos_ref[C]
    for block in range(4):
        att = att_ref[:, :, 512 * block : 512 * block + 512].reshape(512, 512)
        sum_ref[...] = dot(att, grads, TN).reshape(4, 4, 2, 16, 512)
        for zh in range(4):
            keep_ref[block, :, zh] = sum_ref[zh, :, c]
            send_ref[block, :, zh] = sum_ref[zh, :, 1 - c]


def output_kernel(pos_ref, a0, a1, a2, a3, mine_ref, other_ref, out_ref, w_ref, att_ref, wide_ref, sems):
    pairs = [(ref, att_ref.at[step]) for step, ref in enumerate((a0, a1, a2, a3))]
    for core, ref in enumerate((mine_ref, other_ref)):
        c = pos_ref[C] if core == 0 else 1 - pos_ref[C]
        pairs += [(ref.at[:, :, pos_ref[S], zh], w_ref.at[:, zh, :, c]) for zh in range(4)]
    wait_all(run_copies(pairs, sems))
    rows = dot(att_ref[...].reshape(512, 2048), w_ref[...].reshape(2048, 512), NN).reshape(4, 16, 8, 512)
    for step in range(4):
        pixels = pl.ds(pl.multiple_of(wrap(pos_ref[S], 4 - step) * 8, 8), 8)
        wide_ref[:, pixels, :] = rows[step]
    out_ref[...] = wide_ref[...].astype(BF)


def call(kernel, name, out_shape, inputs, out_spec, scratch, mib):
    return pl.pallas_call(
        kernel,
        out_shape=out_shape,
        in_specs=[SMEM] + [ANY] * (len(inputs) - 1),
        out_specs=jax.tree.map(lambda _: out_spec, out_shape),
        scratch_shapes=scratch,
        compiler_params=params(mib),
        name=name,
    )(*inputs)


def per_device(query_frames, key_frames, value_frames, out_weight, out_grad):
    pos = jnp.stack([lax.axis_index(a) for a in DEVICES]).astype(jnp.int32)
    swap = [(0, 1), (1, 0)]
    dma = pltpu.SemaphoreType.DMA

    spread = jnp.broadcast_to(out_weight[None], (16, 16, 512))
    column = lax.all_to_all(spread, ("s", "zh"), 0, 0)

    parcel = jax.ShapeDtypeStruct((4, 32, 2048), BF)
    sent = call(
        pack_kernel, "pack", [parcel] * 4, (pos, query_frames, key_frames, value_frames, out_grad), VMEM,
        [pltpu.VMEM((3, 4, 32, 2048), BF), pltpu.VMEM((16, 32, 512), BF), pltpu.VMEM((4, 4, 32, 512), F32), dma((4,))], 32,
    )
    column, sent = lax.optimization_barrier((column, sent))
    arrived = [sent[0]] + [shift(sent[n], "s", n) for n in (1, 2, 3)]
    mine = lax.all_gather(column.reshape(256, 512), ("x", "y"), axis=0, tiled=True).reshape(4, 4, 4, 4, 16, 512)

    attended = call(
        forward_kernel, "forward", jax.ShapeDtypeStruct((128, 2048), BF), (pos, *arrived), VMEM,
        [pltpu.VMEM((3, 4, 32, 2048), BF), dma((4,))], 24,
    )
    attended_all = [attended] + [shift(attended, "s", n) for n in (1, 2, 3)]
    mine, attended_all[1] = lax.optimization_barrier((mine, attended_all[1]))
    other = lax.ppermute(mine, "c", swap)

    back = call(
        backward_kernel, "backward", [jax.ShapeDtypeStruct((3, 32, 2048), BF)] * 4, (pos, *arrived, mine, other), ANY,
        [
            pltpu.VMEM((4, 4, 4, 4, 2, 16, 512), BF),
            pltpu.VMEM((3, 4, 32, 2048), BF),
            pltpu.VMEM((4, 32, 2048), BF),
            pltpu.VMEM((128, 2048), BF),
            dma((52,)),
            dma((4,)),
        ],
        40,
    )
    *back, attended_all[0] = lax.optimization_barrier((*back, attended_all[0]))
    home = [back[0]] + [shift(back[n], "s", n) for n in (1, 2, 3)]

    quarter = jax.ShapeDtypeStruct((4, 4, 4, 16, 512), F32)
    keep, send = call(
        weight_kernel, "weight", [quarter] * 2, (pos, *attended_all, *sent), VMEM,
        [
            pltpu.VMEM((4, 128, 2048), BF),
            pltpu.VMEM((4, 4, 32, 512), BF),
            pltpu.VMEM((4, 4, 2, 16, 512), F32),
            dma((20,)),
        ],
        32,
    )
    chip_sum = keep + lax.ppermute(send, "c", swap)
    parts = lax.all_to_all(chip_sum.reshape(16, 4, 16, 512), ("x", "y"), 0, 0)

    block_out = call(
        output_kernel, "project", jax.ShapeDtypeStruct((16, 32, 512), BF), (pos, *attended_all, mine, other), VMEM,
        [
            pltpu.VMEM((4, 4, 4, 2, 16, 512), BF),
            pltpu.VMEM((4, 128, 2048), BF),
            pltpu.VMEM((16, 32, 512), F32),
            dma((12,)),
        ],
        32,
    )
    query_grad, key_grad, value_grad = call(
        unpack_kernel, "unpack", [jax.ShapeDtypeStruct((4, 32, 2048), BF)] * 3, (pos, *home), VMEM,
        [pltpu.VMEM((4, 3, 32, 2048), BF), pltpu.VMEM((4, 4, 32, 512), F32), dma((4,))], 32,
    )
    parts, block_out = lax.optimization_barrier((parts, block_out))
    plane_sum = parts.sum(axis=0)
    weight_grad = None
    for step in range(4):
        part = lax.dynamic_index_in_dim(plane_sum, wrap(pos[ZH], step), 0, keepdims=False)
        got = part if step == 0 else shift(part, "zh", step)
        weight_grad = got if weight_grad is None else weight_grad + got
    return block_out, query_grad, key_grad, value_grad, weight_grad


def solution(mesh):
    fine = Mesh(mesh.devices.reshape(4, 4, 4, 2, 4), ("x", "zh", "y", "c", "s"))
    fsdp = ("x", "zh", "y", "c")
    return jax.shard_map(
        per_device,
        mesh=fine,
        in_specs=(
            P("s", fsdp, None),
            P("s", fsdp, None),
            P("s", fsdp, None),
            P(fsdp, "s"),
            P(None, fsdp, "s"),
        ),
        out_specs=(
            P(None, fsdp, "s"),
            P("s", fsdp, None),
            P("s", fsdp, None),
            P("s", fsdp, None),
            P(fsdp, "s"),
        ),
        check_vma=False,
    )
```

```python
import functools
import math

import jax
import jax.numpy as jnp
from jax import lax
from jax.experimental import pallas as pl
from jax.experimental.pallas import tpu as pltpu
from jax.sharding import Mesh
from jax.sharding import PartitionSpec as P

HD = 128
SCALE = 1.0 / math.sqrt(HD)
BF = jnp.bfloat16
F32 = jnp.float32
VMEM = pl.BlockSpec(memory_space=pltpu.VMEM)
SMEM = pl.BlockSpec(memory_space=pltpu.SMEM)
ANY = pl.BlockSpec(memory_space=pl.ANY)
NT = (((1,), (1,)), ((), ()))
TN = (((0,), (0,)), ((), ()))
NN = (((1,), (0,)), ((), ()))
X, ZH, Y, C, S = range(5)
DEVICES = ("x", "zh", "y", "c", "s")


def dot(a, b, dims):
    return lax.dot_general(a, b, dims, preferred_element_type=F32)


def shift(array, axis, step):
    return lax.ppermute(array, axis, [(i, (i + step) % 4) for i in range(4)])


def params(mib):
    return pltpu.CompilerParams(vmem_limit_bytes=mib * 2**20)


def wrap(index, step):
    return lax.rem(index + step, 4)


def run_copies(pairs, sems):
    copies = [pltpu.make_async_copy(src, dst, sems.at[n]) for n, (src, dst) in enumerate(pairs)]
    for copy in copies:
        copy.start()
    return copies


def wait_all(copies):
    for copy in copies:
        copy.wait()


def pack_kernel(pos_ref, q_ref, k_ref, v_ref, g_ref, o0, o1, o2, o3, rows_ref, grad_ref, wide_ref, sems):
    pairs = [(ref, rows_ref.at[which]) for which, ref in enumerate((q_ref, k_ref, v_ref))]
    copies = run_copies(pairs + [(g_ref, grad_ref)], sems)
    for which in range(4):
        copies[which].wait()
        for part in range(4):
            lanes = slice(512 * part, 512 * part + 512)
            block = rows_ref[which, :, :, lanes] if which < 3 else grad_ref[4 * part : 4 * part + 4]
            wide_ref[part] = block.astype(F32)
            for step, out in enumerate((o0, o1, o2, o3)):
                pixels = pl.ds(pl.multiple_of(wrap(pos_ref[S], step) * 8, 8), 8)
                out[which, :, lanes] = wide_ref[part, :, pixels, :].reshape(32, 512).astype(BF)


def unpack_kernel(pos_ref, h0, h1, h2, h3, q_ref, k_ref, v_ref, rows_ref, wide_ref, sems):
    copies = run_copies([(ref, rows_ref.at[step]) for step, ref in enumerate((h0, h1, h2, h3))], sems)
    wait_all(copies)
    for which, out in enumerate((q_ref, k_ref, v_ref)):
        for part in range(4):
            lanes = slice(512 * part, 512 * part + 512)
            for step in range(4):
                pixels = pl.ds(pl.multiple_of(wrap(pos_ref[S], 4 - step) * 8, 8), 8)
                wide_ref[part, :, pixels, :] = rows_ref[step, which, :, lanes].astype(F32).reshape(4, 8, 512)
            out[:, :, lanes] = wide_ref[part].astype(BF)


def allowed_pairs():
    row = lax.broadcasted_iota(jnp.int32, (128, 128), 0)
    col = lax.broadcasted_iota(jnp.int32, (128, 128), 1)
    return ((row & 7) == (col & 7)) & (col <= row)


def softmax_heads(qs, ks, allowed):
    scores = [jnp.where(allowed, dot(q, k, NT) * SCALE, -1e30) for q, k in zip(qs, ks)]
    peaks = [jnp.max(s, axis=-1, keepdims=True) for s in scores]
    terms = [jnp.exp(s - p) for s, p in zip(scores, peaks)]
    sums = [jnp.sum(t, axis=-1, keepdims=True) for t in terms]
    return [t / s for t, s in zip(terms, sums)]


def heads_of(all_ref, which, heads):
    return [all_ref[which, :, :, 128 * h : 128 * h + 128].reshape(128, 128) for h in heads]


def inputs_of(pos_ref, pieces, all_ref):
    return [(ref.at[0:3], all_ref.at[:, wrap(pos_ref[S], 4 - step)]) for step, ref in enumerate(pieces)]


def forward_kernel(pos_ref, e0, e1, e2, e3, att_ref, all_ref, sems):
    wait_all(run_copies(inputs_of(pos_ref, (e0, e1, e2, e3), all_ref), sems))
    allowed = allowed_pairs()
    for block in range(4):
        heads = [4 * block + i for i in range(4)]
        qs, ks, vs = (heads_of(all_ref, which, heads) for which in range(3))
        weights = softmax_heads(qs, ks, allowed)
        for h, w, v in zip(heads, weights, vs):
            att_ref[:, 128 * h : 128 * h + 128] = dot(w.astype(BF), v, NN).astype(BF)


def backward_kernel(
    pos_ref, e0, e1, e2, e3, mine_ref, other_ref, f0, f1, f2, f3, w_ref, all_ref, grad_ref, ag_ref, sems, out_sems
):
    pieces = (e0, e1, e2, e3)
    pairs = []
    for core, ref in enumerate((mine_ref, other_ref)):
        c = pos_ref[C] if core == 0 else 1 - pos_ref[C]
        pairs += [(ref.at[:, :, s, zh], w_ref.at[s, :, zh, :, c]) for s in range(4) for zh in range(4)]
    for step, ref in enumerate(pieces):
        lanes = pl.ds(pl.multiple_of(wrap(pos_ref[S], 4 - step) * 512, 512), 512)
        pairs += [(ref.at[3, :, 512 * g : 512 * g + 512], grad_ref.at[g, :, lanes]) for g in range(4)]
    pairs += inputs_of(pos_ref, pieces, all_ref)
    wait_all(run_copies(pairs, sems))
    total = None
    for s in range(4):
        rows = grad_ref[:, :, 512 * s : 512 * s + 512].reshape(128, 512)
        part = dot(rows, w_ref[s].reshape(2048, 512), NT)
        total = part if total is None else total + part
    ag_ref[...] = total.astype(BF)
    allowed = allowed_pairs()
    for block in range(4):
        heads = [4 * block + i for i in range(4)]
        qs, ks, vs = (heads_of(all_ref, which, heads) for which in range(3))
        gs = [ag_ref[:, 128 * h : 128 * h + 128] for h in heads]
        weights = softmax_heads(qs, ks, allowed)
        wgrads = [dot(g, v, NT) for g, v in zip(gs, vs)]
        dvs = [dot(w.astype(BF), g, TN) for w, g in zip(weights, gs)]
        means = [jnp.sum(w * d, axis=-1, keepdims=True) for w, d in zip(weights, wgrads)]
        sgrads = [(w * (d - m) * SCALE).astype(BF) for w, d, m in zip(weights, wgrads, means)]
        dqs = [dot(d, k, NN) for d, k in zip(sgrads, ks)]
        dks = [dot(d, q, TN) for d, q in zip(sgrads, qs)]
        for which, grads in enumerate((dqs, dks, dvs)):
            for h, grad in zip(heads, grads):
                all_ref[which, :, :, 128 * h : 128 * h + 128] = grad.astype(BF).reshape(4, 32, 128)
    pairs = [(all_ref.at[:, wrap(pos_ref[S], step)], out) for step, out in enumerate((f0, f1, f2, f3))]
    wait_all(run_copies(pairs, out_sems))


def weight_kernel(pos_ref, a0, a1, a2, a3, p0, p1, p2, p3, keep_ref, send_ref, att_ref, grad_ref, sum_ref, sems):
    pairs = [(ref, att_ref.at[step]) for step, ref in enumerate((a0, a1, a2, a3))]
    for step, ref in enumerate((p0, p3, p2, p1)):
        pairs += [(ref.at[3, :, 512 * g : 512 * g + 512], grad_ref.at[step, g]) for g in range(4)]
    wait_all(run_copies(pairs, sems))
    grads = grad_ref[...].reshape(512, 512)
    c = pos_ref[C]
    for block in range(4):
        att = att_ref[:, :, 512 * block : 512 * block + 512].reshape(512, 512)
        sum_ref[...] = dot(att, grads, TN).reshape(4, 4, 2, 16, 512)
        for zh in range(4):
            keep_ref[block, :, zh] = sum_ref[zh, :, c]
            send_ref[block, :, zh] = sum_ref[zh, :, 1 - c]


def output_kernel(pos_ref, a0, a1, a2, a3, mine_ref, other_ref, out_ref, w_ref, att_ref, wide_ref, sems):
    pairs = [(ref, att_ref.at[step]) for step, ref in enumerate((a0, a1, a2, a3))]
    for core, ref in enumerate((mine_ref, other_ref)):
        c = pos_ref[C] if core == 0 else 1 - pos_ref[C]
        pairs += [(ref.at[:, :, pos_ref[S], zh], w_ref.at[:, zh, :, c]) for zh in range(4)]
    wait_all(run_copies(pairs, sems))
    rows = dot(att_ref[...].reshape(512, 2048), w_ref[...].reshape(2048, 512), NN).reshape(4, 16, 8, 512)
    for step in range(4):
        pixels = pl.ds(pl.multiple_of(wrap(pos_ref[S], 4 - step) * 8, 8), 8)
        wide_ref[:, pixels, :] = rows[step]
    out_ref[...] = wide_ref[...].astype(BF)


def call(kernel, name, out_shape, inputs, out_spec, scratch, mib):
    return pl.pallas_call(
        kernel,
        out_shape=out_shape,
        in_specs=[SMEM] + [ANY] * (len(inputs) - 1),
        out_specs=jax.tree.map(lambda _: out_spec, out_shape),
        scratch_shapes=scratch,
        compiler_params=params(mib),
        name=name,
    )(*inputs)


def per_device(query_frames, key_frames, value_frames, out_weight, out_grad):
    pos = jnp.stack([lax.axis_index(a) for a in DEVICES]).astype(jnp.int32)
    swap = [(0, 1), (1, 0)]
    dma = pltpu.SemaphoreType.DMA

    spread = jnp.broadcast_to(out_weight[None], (16, 16, 512))
    column = lax.all_to_all(spread, ("s", "zh"), 0, 0)

    parcel = jax.ShapeDtypeStruct((4, 32, 2048), BF)
    sent = call(
        pack_kernel, "pack", [parcel] * 4, (pos, query_frames, key_frames, value_frames, out_grad), VMEM,
        [pltpu.VMEM((3, 4, 32, 2048), BF), pltpu.VMEM((16, 32, 512), BF), pltpu.VMEM((4, 4, 32, 512), F32), dma((4,))], 32,
    )
    first = shift(sent[1], "s", 1)
    column, two, three = lax.optimization_barrier((column, sent[2], sent[3]))
    column, first = lax.optimization_barrier((column, first))
    arrived = [sent[0], first, shift(two, "s", 2), shift(three, "s", 3)]
    mine = lax.all_gather(column.reshape(256, 512), ("x", "y"), axis=0, tiled=True).reshape(4, 4, 4, 4, 16, 512)

    attended = call(
        forward_kernel, "forward", jax.ShapeDtypeStruct((128, 2048), BF), (pos, *arrived), VMEM,
        [pltpu.VMEM((3, 4, 32, 2048), BF), dma((4,))], 24,
    )
    attended_all = [attended] + [shift(attended, "s", n) for n in (1, 2, 3)]
    mine, attended_all[2] = lax.optimization_barrier((mine, attended_all[2]))
    other = lax.ppermute(mine, "c", swap)

    back = call(
        backward_kernel, "backward", [jax.ShapeDtypeStruct((3, 32, 2048), BF)] * 4, (pos, *arrived, mine, other), ANY,
        [
            pltpu.VMEM((4, 4, 4, 4, 2, 16, 512), BF),
            pltpu.VMEM((3, 4, 32, 2048), BF),
            pltpu.VMEM((4, 32, 2048), BF),
            pltpu.VMEM((128, 2048), BF),
            dma((52,)),
            dma((4,)),
        ],
        40,
    )
    *back, attended_all[0] = lax.optimization_barrier((*back, attended_all[0]))
    home = [back[0]] + [shift(back[n], "s", n) for n in (1, 2, 3)]

    quarter = jax.ShapeDtypeStruct((4, 4, 4, 16, 512), F32)
    keep, send = call(
        weight_kernel, "weight", [quarter] * 2, (pos, *attended_all, *sent), VMEM,
        [
            pltpu.VMEM((4, 128, 2048), BF),
            pltpu.VMEM((4, 4, 32, 512), BF),
            pltpu.VMEM((4, 4, 2, 16, 512), F32),
            dma((20,)),
        ],
        32,
    )
    chip_sum = keep + lax.ppermute(send, "c", swap)
    parts = lax.all_to_all(chip_sum.reshape(16, 4, 16, 512), ("x", "y"), 0, 0)

    block_out = call(
        output_kernel, "project", jax.ShapeDtypeStruct((16, 32, 512), BF), (pos, *attended_all, mine, other), VMEM,
        [
            pltpu.VMEM((4, 4, 4, 2, 16, 512), BF),
            pltpu.VMEM((4, 128, 2048), BF),
            pltpu.VMEM((16, 32, 512), F32),
            dma((12,)),
        ],
        32,
    )
    query_grad, key_grad, value_grad = call(
        unpack_kernel, "unpack", [jax.ShapeDtypeStruct((4, 32, 2048), BF)] * 3, (pos, *home), VMEM,
        [pltpu.VMEM((4, 3, 32, 2048), BF), pltpu.VMEM((4, 4, 32, 512), F32), dma((4,))], 32,
    )
    parts, block_out = lax.optimization_barrier((parts, block_out))
    plane_sum = parts.sum(axis=0)
    weight_grad = None
    for step in range(4):
        part = lax.dynamic_index_in_dim(plane_sum, wrap(pos[ZH], step), 0, keepdims=False)
        got = part if step == 0 else shift(part, "zh", step)
        weight_grad = got if weight_grad is None else weight_grad + got
    return block_out, query_grad, key_grad, value_grad, weight_grad


def solution(mesh):
    fine = Mesh(mesh.devices.reshape(4, 4, 4, 2, 4), ("x", "zh", "y", "c", "s"))
    fsdp = ("x", "zh", "y", "c")
    return jax.shard_map(
        per_device,
        mesh=fine,
        in_specs=(
            P("s", fsdp, None),
            P("s", fsdp, None),
            P("s", fsdp, None),
            P(fsdp, "s"),
            P(None, fsdp, "s"),
        ),
        out_specs=(
            P(None, fsdp, "s"),
            P("s", fsdp, None),
            P("s", fsdp, None),
            P("s", fsdp, None),
            P(fsdp, "s"),
        ),
        check_vma=False,
    )
```

```python
import functools
import math

import jax
import jax.numpy as jnp
from jax import lax
from jax.experimental import pallas as pl
from jax.experimental.pallas import tpu as pltpu
from jax.sharding import Mesh
from jax.sharding import PartitionSpec as P

HD = 128
SCALE = 1.0 / math.sqrt(HD)
BF = jnp.bfloat16
F32 = jnp.float32
VMEM = pl.BlockSpec(memory_space=pltpu.VMEM)
SMEM = pl.BlockSpec(memory_space=pltpu.SMEM)
ANY = pl.BlockSpec(memory_space=pl.ANY)
NT = (((1,), (1,)), ((), ()))
TN = (((0,), (0,)), ((), ()))
NN = (((1,), (0,)), ((), ()))
X, ZH, Y, C, S = range(5)
DEVICES = ("x", "zh", "y", "c", "s")


def dot(a, b, dims):
    return lax.dot_general(a, b, dims, preferred_element_type=F32)


def shift(array, axis, step):
    return lax.ppermute(array, axis, [(i, (i + step) % 4) for i in range(4)])


def params(mib):
    return pltpu.CompilerParams(vmem_limit_bytes=mib * 2**20)


def wrap(index, step):
    return lax.rem(index + step, 4)


def run_copies(pairs, sems):
    copies = [pltpu.make_async_copy(src, dst, sems.at[n]) for n, (src, dst) in enumerate(pairs)]
    for copy in copies:
        copy.start()
    return copies


def wait_all(copies):
    for copy in copies:
        copy.wait()


def pack_kernel(
    pos_ref, q_ref, k_ref, v_ref, g_ref, o0, o1, o2, o3, stay_ref, rows_ref, grad_ref, wide_ref, sems
):
    pairs = [(ref, rows_ref.at[which]) for which, ref in enumerate((q_ref, k_ref, v_ref))]
    copies = run_copies(pairs + [(g_ref, grad_ref)], sems)
    for which in range(4):
        copies[which].wait()
        for part in range(4):
            lanes = slice(512 * part, 512 * part + 512)
            block = rows_ref[which, :, :, lanes] if which < 3 else grad_ref[4 * part : 4 * part + 4]
            wide_ref[part] = block.astype(F32)
            for step, out in enumerate((o0, o1, o2, o3)):
                pixels = pl.ds(pl.multiple_of(wrap(pos_ref[S], step) * 8, 8), 8)
                rows = wide_ref[part, :, pixels, :].reshape(32, 512).astype(BF)
                out[which, :, lanes] = rows
                if which == 3:
                    stay_ref[step, part] = rows


def unpack_kernel(pos_ref, h0, h1, h2, h3, q_ref, k_ref, v_ref, rows_ref, wide_ref, sems):
    copies = run_copies([(ref, rows_ref.at[step]) for step, ref in enumerate((h0, h1, h2, h3))], sems)
    wait_all(copies)
    for which, out in enumerate((q_ref, k_ref, v_ref)):
        for part in range(4):
            lanes = slice(512 * part, 512 * part + 512)
            for step in range(4):
                pixels = pl.ds(pl.multiple_of(wrap(pos_ref[S], 4 - step) * 8, 8), 8)
                wide_ref[part, :, pixels, :] = rows_ref[step, which, :, lanes].astype(F32).reshape(4, 8, 512)
            out[:, :, lanes] = wide_ref[part].astype(BF)


def allowed_pairs():
    row = lax.broadcasted_iota(jnp.int32, (128, 128), 0)
    col = lax.broadcasted_iota(jnp.int32, (128, 128), 1)
    return ((row & 7) == (col & 7)) & (col <= row)


def softmax_heads(qs, ks, allowed):
    scores = [jnp.where(allowed, dot(q, k, NT) * SCALE, -1e30) for q, k in zip(qs, ks)]
    peaks = [jnp.max(s, axis=-1, keepdims=True) for s in scores]
    terms = [jnp.exp(s - p) for s, p in zip(scores, peaks)]
    sums = [jnp.sum(t, axis=-1, keepdims=True) for t in terms]
    return [t / s for t, s in zip(terms, sums)]


def heads_of(all_ref, which, heads):
    return [all_ref[which, :, :, 128 * h : 128 * h + 128].reshape(128, 128) for h in heads]


def inputs_of(pos_ref, pieces, all_ref):
    return [(ref.at[0:3], all_ref.at[:, wrap(pos_ref[S], 4 - step)]) for step, ref in enumerate(pieces)]


def forward_kernel(pos_ref, e0, e1, e2, e3, att_ref, all_ref, sems):
    wait_all(run_copies(inputs_of(pos_ref, (e0, e1, e2, e3), all_ref), sems))
    allowed = allowed_pairs()
    for block in range(4):
        heads = [4 * block + i for i in range(4)]
        qs, ks, vs = (heads_of(all_ref, which, heads) for which in range(3))
        weights = softmax_heads(qs, ks, allowed)
        for h, w, v in zip(heads, weights, vs):
            att_ref[:, 128 * h : 128 * h + 128] = dot(w.astype(BF), v, NN).astype(BF)


def backward_kernel(
    pos_ref, e0, e1, e2, e3, mine_ref, other_ref, f0, f1, f2, f3, w_ref, all_ref, grad_ref, ag_ref, sems, out_sems
):
    pieces = (e0, e1, e2, e3)
    pairs = []
    for core, ref in enumerate((mine_ref, other_ref)):
        c = pos_ref[C] if core == 0 else 1 - pos_ref[C]
        pairs += [(ref.at[:, :, s, zh], w_ref.at[s, :, zh, :, c]) for s in range(4) for zh in range(4)]
    for step, ref in enumerate(pieces):
        lanes = pl.ds(pl.multiple_of(wrap(pos_ref[S], 4 - step) * 512, 512), 512)
        pairs += [(ref.at[3, :, 512 * g : 512 * g + 512], grad_ref.at[g, :, lanes]) for g in range(4)]
    pairs += inputs_of(pos_ref, pieces, all_ref)
    wait_all(run_copies(pairs, sems))
    total = None
    for s in range(4):
        rows = grad_ref[:, :, 512 * s : 512 * s + 512].reshape(128, 512)
        part = dot(rows, w_ref[s].reshape(2048, 512), NT)
        total = part if total is None else total + part
    ag_ref[...] = total.astype(BF)
    allowed = allowed_pairs()
    for block in range(4):
        heads = [4 * block + i for i in range(4)]
        qs, ks, vs = (heads_of(all_ref, which, heads) for which in range(3))
        gs = [ag_ref[:, 128 * h : 128 * h + 128] for h in heads]
        weights = softmax_heads(qs, ks, allowed)
        wgrads = [dot(g, v, NT) for g, v in zip(gs, vs)]
        dvs = [dot(w.astype(BF), g, TN) for w, g in zip(weights, gs)]
        means = [jnp.sum(w * d, axis=-1, keepdims=True) for w, d in zip(weights, wgrads)]
        sgrads = [(w * (d - m) * SCALE).astype(BF) for w, d, m in zip(weights, wgrads, means)]
        dqs = [dot(d, k, NN) for d, k in zip(sgrads, ks)]
        dks = [dot(d, q, TN) for d, q in zip(sgrads, qs)]
        for which, grads in enumerate((dqs, dks, dvs)):
            for h, grad in zip(heads, grads):
                all_ref[which, :, :, 128 * h : 128 * h + 128] = grad.astype(BF).reshape(4, 32, 128)
    pairs = [(all_ref.at[:, wrap(pos_ref[S], step)], out) for step, out in enumerate((f0, f1, f2, f3))]
    wait_all(run_copies(pairs, out_sems))


def weight_kernel(pos_ref, a0, a1, a2, a3, stay_ref, keep_ref, send_ref, att_ref, grad_ref, sum_ref, sems):
    pairs = [(ref, att_ref.at[step]) for step, ref in enumerate((a0, a1, a2, a3))]
    pairs += [(stay_ref.at[(4 - step) % 4], grad_ref.at[step]) for step in range(4)]
    wait_all(run_copies(pairs, sems))
    grads = grad_ref[...].reshape(512, 512)
    c = pos_ref[C]
    for block in range(4):
        att = att_ref[:, :, 512 * block : 512 * block + 512].reshape(512, 512)
        sum_ref[...] = dot(att, grads, TN).reshape(4, 4, 2, 16, 512)
        for zh in range(4):
            keep_ref[block, :, zh] = sum_ref[zh, :, c]
            send_ref[block, :, zh] = sum_ref[zh, :, 1 - c]


def output_kernel(pos_ref, a0, a1, a2, a3, mine_ref, other_ref, out_ref, w_ref, att_ref, wide_ref, sems):
    pairs = [(ref, att_ref.at[step]) for step, ref in enumerate((a0, a1, a2, a3))]
    for core, ref in enumerate((mine_ref, other_ref)):
        c = pos_ref[C] if core == 0 else 1 - pos_ref[C]
        pairs += [(ref.at[:, :, pos_ref[S], zh], w_ref.at[:, zh, :, c]) for zh in range(4)]
    wait_all(run_copies(pairs, sems))
    rows = dot(att_ref[...].reshape(512, 2048), w_ref[...].reshape(2048, 512), NN).reshape(4, 16, 8, 512)
    for step in range(4):
        pixels = pl.ds(pl.multiple_of(wrap(pos_ref[S], 4 - step) * 8, 8), 8)
        wide_ref[:, pixels, :] = rows[step]
    out_ref[...] = wide_ref[...].astype(BF)


def call(kernel, name, out_shape, inputs, out_spec, scratch, mib):
    return pl.pallas_call(
        kernel,
        out_shape=out_shape,
        in_specs=[SMEM] + [ANY] * (len(inputs) - 1),
        out_specs=jax.tree.map(lambda _: out_spec, out_shape),
        scratch_shapes=scratch,
        compiler_params=params(mib),
        name=name,
    )(*inputs)


def per_device(query_frames, key_frames, value_frames, out_weight, out_grad):
    pos = jnp.stack([lax.axis_index(a) for a in DEVICES]).astype(jnp.int32)
    swap = [(0, 1), (1, 0)]
    dma = pltpu.SemaphoreType.DMA

    spread = jnp.broadcast_to(out_weight[None], (16, 16, 512))
    column = lax.all_to_all(spread, ("s", "zh"), 0, 0)

    parcel = jax.ShapeDtypeStruct((4, 32, 2048), BF)
    *sent, stay = call(
        pack_kernel, "pack", [parcel] * 4 + [jax.ShapeDtypeStruct((4, 4, 32, 512), BF)], (pos, query_frames, key_frames, value_frames, out_grad), VMEM,
        [pltpu.VMEM((3, 4, 32, 2048), BF), pltpu.VMEM((16, 32, 512), BF), pltpu.VMEM((4, 4, 32, 512), F32), dma((4,))], 32,
    )
    first = shift(sent[1], "s", 1)
    column, two, three = lax.optimization_barrier((column, sent[2], sent[3]))
    column, first = lax.optimization_barrier((column, first))
    arrived = [sent[0], first, shift(two, "s", 2), shift(three, "s", 3)]
    mine = lax.all_gather(column.reshape(256, 512), ("x", "y"), axis=0, tiled=True).reshape(4, 4, 4, 4, 16, 512)

    attended = call(
        forward_kernel, "forward", jax.ShapeDtypeStruct((128, 2048), BF), (pos, *arrived), VMEM,
        [pltpu.VMEM((3, 4, 32, 2048), BF), dma((4,))], 24,
    )
    attended_all = [attended] + [shift(attended, "s", n) for n in (1, 2, 3)]
    mine, attended_all[2] = lax.optimization_barrier((mine, attended_all[2]))
    other = lax.ppermute(mine, "c", swap)

    back = call(
        backward_kernel, "backward", [jax.ShapeDtypeStruct((3, 32, 2048), BF)] * 4, (pos, *arrived, mine, other), ANY,
        [
            pltpu.VMEM((4, 4, 4, 4, 2, 16, 512), BF),
            pltpu.VMEM((3, 4, 32, 2048), BF),
            pltpu.VMEM((4, 32, 2048), BF),
            pltpu.VMEM((128, 2048), BF),
            dma((52,)),
            dma((4,)),
        ],
        40,
    )
    *back, attended_all[0] = lax.optimization_barrier((*back, attended_all[0]))
    home = [back[0]] + [shift(back[n], "s", n) for n in (1, 2, 3)]

    quarter = jax.ShapeDtypeStruct((4, 4, 4, 16, 512), F32)
    keep, send = call(
        weight_kernel, "weight", [quarter] * 2, (pos, *attended_all, stay), VMEM,
        [
            pltpu.VMEM((4, 128, 2048), BF),
            pltpu.VMEM((4, 4, 32, 512), BF),
            pltpu.VMEM((4, 4, 2, 16, 512), F32),
            dma((20,)),
        ],
        32,
    )
    chip_sum = keep + lax.ppermute(send, "c", swap)
    parts = lax.all_to_all(chip_sum.reshape(16, 4, 16, 512), ("x", "y"), 0, 0)

    block_out = call(
        output_kernel, "project", jax.ShapeDtypeStruct((16, 32, 512), BF), (pos, *attended_all, mine, other), VMEM,
        [
            pltpu.VMEM((4, 4, 4, 2, 16, 512), BF),
            pltpu.VMEM((4, 128, 2048), BF),
            pltpu.VMEM((16, 32, 512), F32),
            dma((12,)),
        ],
        32,
    )
    query_grad, key_grad, value_grad = call(
        unpack_kernel, "unpack", [jax.ShapeDtypeStruct((4, 32, 2048), BF)] * 3, (pos, *home), VMEM,
        [pltpu.VMEM((4, 3, 32, 2048), BF), pltpu.VMEM((4, 4, 32, 512), F32), dma((4,))], 32,
    )
    parts, block_out = lax.optimization_barrier((parts, block_out))
    plane_sum = parts.sum(axis=0)
    weight_grad = lax.all_to_all(plane_sum, "zh", 0, 0).sum(axis=0)
    return block_out, query_grad, key_grad, value_grad, weight_grad


def solution(mesh):
    fine = Mesh(mesh.devices.reshape(4, 4, 4, 2, 4), ("x", "zh", "y", "c", "s"))
    fsdp = ("x", "zh", "y", "c")
    return jax.shard_map(
        per_device,
        mesh=fine,
        in_specs=(
            P("s", fsdp, None),
            P("s", fsdp, None),
            P("s", fsdp, None),
            P(fsdp, "s"),
            P(None, fsdp, "s"),
        ),
        out_specs=(
            P(None, fsdp, "s"),
            P("s", fsdp, None),
            P("s", fsdp, None),
            P("s", fsdp, None),
            P(fsdp, "s"),
        ),
        check_vma=False,
    )
```
